512 devices in a mesh: dp: 16 (over x, y_lo), tensor: 32 (over z, y_hi, core).
Axes of the slice: x: 4, y: 8 (y_hi: 2, y_lo: 4; y = y_hi * 4 + y_lo), z: 8, core: 2. Of those that a mesh axis runs over, the one named last changes fastest.
Arguments:
- out_grad: bfloat16 [12288, 8192], P(('dp', 'tensor')), may hold values from -0.01953125 to 0.01953125
- hidden: bfloat16 [12288, 28672], P('dp', 'tensor'), may hold values from -6 to 6
- projector: bfloat16 [8192, 1024], P('dp'), may hold values from -0.1875 to 0.1875
- moment_one: float32 [1024, 28672], P('dp', 'tensor'), may hold values from -3 to 3
- moment_two: float32 [1024, 28672], P('dp', 'tensor'), may hold values from 0.1 to 2
Outputs:
- update: bfloat16 [28672, 8192], P('tensor', 'dp')
- new_one: float32 [1024, 28672], P('dp', 'tensor')
- new_two: float32 [1024, 28672], P('dp', 'tensor')
The draws below stay inside these ranges and needn't reach their ends.
All inputs are finite; a program needn't handle non-finite values.
Results may differ from the reference program's by a relative error of at most 0.018.
Values may be sent and summed in bfloat16 or wider, within the bound.
No kernel may reach another device: no remote copies, remote signals or barrier semaphores. Data moves between devices by JAX's collectives and lax.ppermute only.
A program may use at most 64 MiB of HBM per device.

```python
import math
import jax
import jax.numpy as jnp
from jax import lax

D = 8192
FF = 28672
RANK = 1024
STEP = 1000
TOK_DEV = 768
TOKENS = 12288
N_DP = 16


def steps_of(own_key, extent, split, smallest, top_value):
    def one(axis_at, shards_of):
        draws = jax.random.uniform(jax.random.fold_in(jax.random.fold_in(own_key, 6), axis_at), (shards_of,), jnp.float32, smallest / len(split), top_value / len(split))
        return jnp.repeat(jnp.exp(draws), extent[axis_at] // shards_of).reshape((-1,) + (1,) * (len(extent) - axis_at - 1))

    gain = one(*split[0])
    for cut in split[1:]:
        gain = gain * one(*cut)
    return gain


def gaussian(rng, shape, deviation, limit, pieces=(), held_as=jnp.bfloat16):
    result = jax.random.normal(rng, shape, jnp.float32) * deviation
    if len(pieces) > 0:
        result = steps_of(rng, shape, pieces, -0.22, 0.18) * result
    return jnp.clip(result, min=-limit, max=limit).astype(held_as)


def setup_inputs(seed: int = 0) -> dict:
    keys = jax.random.split(jax.random.key(seed), 6)
    return {
        "out_grad": gaussian(keys[0], (TOKENS, D), (8 * TOKENS) ** -0.5, 0.01953125, ((0, 512),)),
        "hidden": gaussian(keys[1], (TOKENS, FF), 1.0, 6.0, ((0, 16), (1, 32))),
        "projector": gaussian(keys[2], (D, RANK), RANK ** -0.5, 0.1875, ((0, 16),)),
        "moment_one": gaussian(keys[3], (RANK, FF), 0.5, 3.0, ((0, 16), (1, 32)), jnp.float32),
        "moment_two": jnp.clip(jnp.exp(math.log(2.0) - 2.9957323 * jax.random.uniform(keys[4], (RANK, FF), jnp.float32) ** steps_of(keys[4], (RANK, FF), ((0, 16), (1, 32)), -0.2, 0.2)), 0.1, 2.0),
    }


def reference(out_grad, hidden, projector, moment_one, moment_two):
    block = D // N_DP
    total = jnp.zeros((TOKENS, RANK), jnp.float32)
    for index in range(N_DP):
        cols = out_grad[:, index * block:(index + 1) * block].astype(jnp.float32)
        rows = projector[index * block:(index + 1) * block, :].astype(jnp.float32)
        partial_term = lax.optimization_barrier(jnp.dot(cols, rows).astype(jnp.bfloat16))
        total = total + partial_term.astype(jnp.float32)
    projected = total.astype(jnp.bfloat16)
    rank_grad = jnp.zeros((RANK, FF), jnp.float32)
    for index in range(N_DP):
        left = projected[index * TOK_DEV:(index + 1) * TOK_DEV, :].astype(jnp.float32)
        right = hidden[index * TOK_DEV:(index + 1) * TOK_DEV, :].astype(jnp.float32)
        group_term = lax.optimization_barrier(jnp.dot(left.T, right).astype(jnp.bfloat16))
        rank_grad = rank_grad + group_term.astype(jnp.float32)
    new_one = 0.9 * moment_one + 0.1 * rank_grad
    new_two = 0.999 * moment_two + 0.001 * rank_grad * rank_grad
    first_hat = new_one / (1.0 - 0.9 ** STEP)
    second_hat = new_two / (1.0 - 0.999 ** STEP)
    normalized = (first_hat / (jnp.sqrt(second_hat) + 1e-08)).astype(jnp.bfloat16)
    update = jnp.dot(normalized.astype(jnp.float32).T, projector.astype(jnp.float32).T)
    return (update.astype(jnp.bfloat16), new_one, new_two)
```

```python
import jax
import jax.numpy as jnp
from jax import lax
from jax.sharding import Mesh
from jax.sharding import PartitionSpec as P

STEP = 1000

DP = ("x", "yl")
TENSOR = ("z", "yh", "c")


def adam_moments(rank_grad, moment_one, moment_two):
    new_one = 0.9 * moment_one + 0.1 * rank_grad
    new_two = 0.999 * moment_two + 0.001 * rank_grad * rank_grad
    first_hat = new_one / (1.0 - 0.9**STEP)
    second_hat = new_two / (1.0 - 0.999**STEP)
    normalized = (first_hat / (jnp.sqrt(second_hat) + 1e-08)).astype(jnp.bfloat16)
    return (normalized, new_one, new_two)


def exchange(parts, axis):
    return lax.all_to_all(parts, axis, 0, 0)


def summed(parts):
    return jnp.sum(parts.astype(jnp.float32), axis=0)


def shards(out_grad, hidden, projector, moment_one, moment_two):
    n_dp = lax.axis_size(DP)
    n_x, n_yl = lax.axis_size("x"), lax.axis_size("yl")
    n_zy = lax.axis_size(("z", "yh"))
    rows, width = out_grad.shape
    block, rank = projector.shape
    own_rows, columns = moment_one.shape

    pieces = exchange(out_grad.reshape(rows, n_dp, block).swapaxes(0, 1), DP)
    partial = jnp.dot(
        pieces.reshape(n_dp * rows, block), projector, preferred_element_type=jnp.float32
    ).astype(jnp.bfloat16)
    own = summed(exchange(partial.reshape(n_dp, rows, rank), DP)).astype(jnp.bfloat16)

    mine = exchange(jnp.broadcast_to(own, (n_zy, rows, rank)), ("z", "yh"))
    other = lax.ppermute(mine, "c", [(0, 1), (1, 0)])
    core = lax.axis_index("c")
    tokens = hidden.reshape(n_zy, 2, rows, columns)
    group = jnp.zeros((rank, columns), jnp.float32)
    for left, at in ((mine, core), (other, 1 - core)):
        right = lax.dynamic_index_in_dim(tokens, at, 1, keepdims=False)
        group = group + lax.dot_general(
            left.reshape(n_zy * rows, rank),
            right.reshape(n_zy * rows, columns),
            (((0,), (0,)), ((), ())),
            preferred_element_type=jnp.float32,
        )
    group = group.astype(jnp.bfloat16)

    along_x = summed(exchange(group.reshape(n_x, rank // n_x, columns), "x")).astype(jnp.bfloat16)
    rank_grad = summed(exchange(along_x.reshape(n_yl, own_rows, columns), "yl"))

    normalized, new_one, new_two = adam_moments(rank_grad, moment_one, moment_two)

    quarter = exchange(jnp.broadcast_to(normalized, (n_yl, own_rows, columns)), "yl")
    quarter = quarter.reshape(n_yl * own_rows, columns)
    full = exchange(jnp.broadcast_to(quarter, (n_x,) + quarter.shape), "x").reshape(rank, columns)
    update = lax.dot_general(
        full, projector, (((0,), (1,)), ((), ())), preferred_element_type=jnp.float32
    )
    return (update.astype(jnp.bfloat16), new_one, new_two)


def solution(mesh):
    fine = Mesh(mesh.devices.reshape(4, 4, 8, 2, 2), DP + TENSOR)
    in_specs = (
        P(DP + TENSOR, None),
        P(DP, TENSOR),
        P(DP, None),
        P(DP, TENSOR),
        P(DP, TENSOR),
    )
    out_specs = (P(TENSOR, DP), P(DP, TENSOR), P(DP, TENSOR))
    return jax.shard_map(shards, mesh=fine, in_specs=in_specs, out_specs=out_specs, check_vma=False)
```

```python
import jax
import jax.numpy as jnp
import numpy as np
from jax import lax
from jax.sharding import Mesh
from jax.sharding import PartitionSpec as P

STEP = 1000

DP = ("x", "yl")
TENSOR = ("z", "yh", "c")
SIZES = (4, 4, 8, 2, 2)


def adam_moments(rank_grad, moment_one, moment_two):
    new_one = 0.9 * moment_one + 0.1 * rank_grad
    new_two = 0.999 * moment_two + 0.001 * rank_grad * rank_grad
    first_hat = new_one / (1.0 - 0.9**STEP)
    second_hat = new_two / (1.0 - 0.999**STEP)
    normalized = (first_hat / (jnp.sqrt(second_hat) + 1e-08)).astype(jnp.bfloat16)
    return (normalized, new_one, new_two)


def exchange(parts, axis):
    return lax.all_to_all(parts, axis, 0, 0)


def groups(axes, order):
    names = DP + TENSOR
    ids = np.arange(np.prod(SIZES)).reshape(SIZES)
    inside = [names.index(a) for a in axes]
    outside = [i for i in range(len(names)) if i not in inside]
    size = int(np.prod([SIZES[i] for i in inside]))
    lists = ids.transpose(outside + inside).reshape(-1, 2, size)
    return np.stack([lists[:, 0], lists[:, 1, order]], axis=1).reshape(-1, size).tolist()


def exchange_in(parts, axes, order):
    return lax.all_to_all(
        parts, DP + TENSOR, 0, 0, axis_index_groups=groups(axes, order), tiled=True
    )


def summed(parts):
    return jnp.sum(parts.astype(jnp.float32), axis=0)


def shards(out_grad, hidden, projector, moment_one, moment_two):
    n_dp = lax.axis_size(DP)
    n_x, n_yl = lax.axis_size("x"), lax.axis_size("yl")
    n_zy = lax.axis_size(("z", "yh"))
    rows, width = out_grad.shape
    block, rank = projector.shape
    own_rows, columns = moment_one.shape
    quarter = rank // n_x

    core = lax.axis_index("c")
    tokens = lax.all_gather(hidden, "x", axis=0, tiled=True)

    pieces = exchange(out_grad.reshape(rows, n_dp, block).swapaxes(0, 1), DP)
    partial = jnp.dot(
        pieces.reshape(n_dp * rows, block), projector, preferred_element_type=jnp.float32
    ).astype(jnp.bfloat16)
    partial = partial.reshape(n_x, n_yl, rows, n_x, quarter).transpose(3, 1, 0, 2, 4)
    own = summed(exchange(partial.reshape(n_dp, n_x * rows, quarter), DP)).astype(jnp.bfloat16)

    mine = jnp.broadcast_to(own, (n_zy, n_x * rows, quarter))
    mine = exchange_in(mine, ("z", "yh"), list(range(n_zy))[::-1])
    other = lax.ppermute(mine, "c", [(0, 1), (1, 0)])
    first = lax.axis_index("c") == 0
    both = jnp.stack([jnp.where(first, mine, other), jnp.where(first, other, mine)[::-1]], axis=1)
    left = both.reshape(n_zy, 2, n_x, rows, quarter).transpose(2, 0, 1, 3, 4)
    group = lax.dot_general(
        left.reshape(tokens.shape[0], quarter),
        tokens,
        (((0,), (0,)), ((), ())),
        preferred_element_type=jnp.float32,
    ).astype(jnp.bfloat16)

    blocks = group.reshape(n_yl, own_rows, columns)
    blocks = jnp.where(core == 0, blocks, jnp.roll(blocks, -2, axis=0))
    blocks = exchange_in(blocks, ("yl",), [2, 3, 0, 1])
    rank_grad = summed(blocks)

    normalized, new_one, new_two = adam_moments(rank_grad, moment_one, moment_two)

    part = lax.all_gather(normalized, "yl", axis=0, tiled=True)
    full = exchange(jnp.broadcast_to(part, (n_x,) + part.shape), "x").reshape(rank, columns)
    update = lax.dot_general(
        full, projector, (((0,), (1,)), ((), ())), preferred_element_type=jnp.float32
    )
    return (update.astype(jnp.bfloat16), new_one, new_two)


def solution(mesh):
    fine = Mesh(mesh.devices.reshape(SIZES), DP + TENSOR)
    in_specs = (
        P(DP + TENSOR, None),
        P(DP, TENSOR),
        P(DP, None),
        P(DP, TENSOR),
        P(DP, TENSOR),
    )
    out_specs = (P(TENSOR, DP), P(DP, TENSOR), P(DP, TENSOR))
    return jax.shard_map(shards, mesh=fine, in_specs=in_specs, out_specs=out_specs, check_vma=False)
```

```python
import jax
import jax.numpy as jnp
import numpy as np
from jax import lax
from jax.experimental import pallas as pl
from jax.experimental.pallas import tpu as pltpu
from jax.sharding import Mesh
from jax.sharding import PartitionSpec as P

STEP = 1000

DP = ("x", "yl")
TENSOR = ("z", "yh", "c")
SIZES = (4, 4, 8, 2, 2)


def adam_moments(rank_grad, moment_one, moment_two):
    new_one = 0.9 * moment_one + 0.1 * rank_grad
    new_two = 0.999 * moment_two + 0.001 * rank_grad * rank_grad
    first_hat = new_one / (1.0 - 0.9**STEP)
    second_hat = new_two / (1.0 - 0.999**STEP)
    normalized = (first_hat / (jnp.sqrt(second_hat) + 1e-08)).astype(jnp.bfloat16)
    return (normalized, new_one, new_two)


def exchange(parts, axis):
    return lax.all_to_all(parts, axis, 0, 0)


def groups(axes, order):
    names = DP + TENSOR
    ids = np.arange(np.prod(SIZES)).reshape(SIZES)
    inside = [names.index(a) for a in axes]
    outside = [i for i in range(len(names)) if i not in inside]
    size = int(np.prod([SIZES[i] for i in inside]))
    lists = ids.transpose(outside + inside).reshape(-1, 2, size)
    return np.stack([lists[:, 0], lists[:, 1, order]], axis=1).reshape(-1, size).tolist()


def exchange_in(parts, axes, order):
    return lax.all_to_all(
        parts, DP + TENSOR, 0, 0, axis_index_groups=groups(axes, order), tiled=True
    )


def turn(i):
    return i // SIZES[1] * SIZES[1] + (i + SIZES[1] // 2) % SIZES[1]


def by_block(out_grad, block):
    rows, width = out_grad.shape
    n = width // block

    def kernel(in_ref, out_ref, sems):
        shift = lax.axis_index("c") * (SIZES[1] // 2)
        copies = []
        for i in range(n):
            at = i // SIZES[1] * SIZES[1] + lax.rem(i + shift, SIZES[1])
            columns = pl.ds(pl.multiple_of(at * block, block), block)
            copies.append(
                pltpu.make_async_copy(in_ref.at[:, columns], out_ref.at[i], sems.at[i])
            )
        for copy in copies:
            copy.start()
        for copy in copies:
            copy.wait()

    return pl.pallas_call(
        kernel,
        in_specs=[pl.BlockSpec(memory_space=pl.ANY)],
        out_specs=pl.BlockSpec(memory_space=pl.ANY),
        out_shape=jax.ShapeDtypeStruct((n, rows, block), out_grad.dtype),
        scratch_shapes=[pltpu.SemaphoreType.DMA((n,))],
        compiler_params=pltpu.CompilerParams(vmem_limit_bytes=2**20),
        cost_estimate=pl.CostEstimate(
            flops=0, bytes_accessed=2 * out_grad.size * out_grad.dtype.itemsize, transcendentals=0
        ),
    )(out_grad)


def by_core(tokens):
    n_x, n_zy, n_c, rows, columns = tokens.shape

    def kernel(in_ref, out_ref, sems):
        copies = [pltpu.make_async_copy(in_ref.at[:, :, 0], out_ref.at[0], sems.at[0])]
        for i in range(n_zy):
            copies.append(
                pltpu.make_async_copy(
                    in_ref.at[:, n_zy - 1 - i, 1], out_ref.at[1, :, i], sems.at[1 + i]
                )
            )
        for copy in copies:
            copy.start()
        for copy in copies:
            copy.wait()

    return pl.pallas_call(
        kernel,
        in_specs=[pl.BlockSpec(memory_space=pl.ANY)],
        out_specs=pl.BlockSpec(memory_space=pl.ANY),
        out_shape=jax.ShapeDtypeStruct((n_c, n_x, n_zy, rows, columns), tokens.dtype),
        scratch_shapes=[pltpu.SemaphoreType.DMA((1 + n_zy,))],
        compiler_params=pltpu.CompilerParams(vmem_limit_bytes=2**20),
        cost_estimate=pl.CostEstimate(
            flops=0, bytes_accessed=2 * tokens.size * tokens.dtype.itemsize, transcendentals=0
        ),
    )(tokens)


def summed(parts):
    return jnp.sum(parts.astype(jnp.float32), axis=0)


def shards(out_grad, hidden, projector, moment_one, moment_two):
    n_dp = lax.axis_size(DP)
    n_x, n_yl = lax.axis_size("x"), lax.axis_size("yl")
    n_zy = lax.axis_size(("z", "yh"))
    rows, width = out_grad.shape
    block, rank = projector.shape
    own_rows, columns = moment_one.shape
    quarter = rank // n_x

    core = lax.axis_index("c")
    tokens = lax.all_gather(hidden, "x", axis=0, tiled=True)

    turned = [turn(i) for i in range(n_dp)]

    pieces = exchange_in(by_block(out_grad, block), DP, turned)
    partial = jnp.dot(
        pieces.reshape(n_dp * rows, block), projector, preferred_element_type=jnp.float32
    ).astype(jnp.bfloat16)
    partial = partial.reshape(n_x, n_yl, rows, n_x, quarter).transpose(3, 1, 0, 2, 4)
    partial = partial.reshape(n_dp, n_x * rows, quarter)
    own = summed(exchange_in(partial, DP, turned)).astype(jnp.bfloat16)

    mine = jnp.broadcast_to(own, (n_zy, n_x * rows, quarter))
    mine = exchange_in(mine, ("z", "yh"), list(range(n_zy))[::-1])
    mine, tokens = lax.optimization_barrier((mine, tokens))
    other = lax.ppermute(mine, "c", [(0, 1), (1, 0)])
    tokens = by_core(tokens.reshape(n_x, n_zy, 2, rows, columns))
    tokens = tokens.reshape(2, n_x, n_zy * rows, columns)
    group = jnp.zeros((quarter, columns), jnp.float32)
    for at, left in ((core, mine), (1 - core, other)):
        left = left.reshape(n_zy, n_x, rows, quarter).swapaxes(0, 1)
        group = group + lax.dot_general(
            left.reshape(n_x, n_zy * rows, quarter),
            lax.dynamic_index_in_dim(tokens, at, 0, keepdims=False),
            (((0, 1), (0, 1)), ((), ())),
            preferred_element_type=jnp.float32,
        )
    group = group.astype(jnp.bfloat16)

    blocks = group.reshape(n_yl, own_rows, columns)
    blocks = jnp.where(core == 0, blocks, jnp.roll(blocks, -2, axis=0))
    blocks = exchange_in(blocks, ("yl",), [2, 3, 0, 1])
    rank_grad = summed(blocks)

    normalized, new_one, new_two = adam_moments(rank_grad, moment_one, moment_two)

    part = lax.all_gather(normalized, "yl", axis=0, tiled=True)
    full = exchange(jnp.broadcast_to(part, (n_x,) + part.shape), "x").reshape(rank, columns)
    update = lax.dot_general(
        full, projector, (((0,), (1,)), ((), ())), preferred_element_type=jnp.float32
    )
    return (update.astype(jnp.bfloat16), new_one, new_two)


def solution(mesh):
    fine = Mesh(mesh.devices.reshape(SIZES), DP + TENSOR)
    in_specs = (
        P(DP + TENSOR, None),
        P(DP, TENSOR),
        P(DP, None),
        P(DP, TENSOR),
        P(DP, TENSOR),
    )
    out_specs = (P(TENSOR, DP), P(DP, TENSOR), P(DP, TENSOR))
    return jax.shard_map(shards, mesh=fine, in_specs=in_specs, out_specs=out_specs, check_vma=False)
```

```python
import jax
import jax.numpy as jnp
import numpy as np
from jax import lax
from jax.experimental import pallas as pl
from jax.experimental.pallas import tpu as pltpu
from jax.sharding import Mesh
from jax.sharding import PartitionSpec as P

STEP = 1000

DP = ("x", "yl")
TENSOR = ("z", "yh", "c")
SIZES = (4, 4, 8, 2, 2)
BY_YH = [z * SIZES[3] + yh for yh in range(SIZES[3]) for z in range(SIZES[2])]


def adam_moments(rank_grad, moment_one, moment_two):
    new_one = 0.9 * moment_one + 0.1 * rank_grad
    new_two = 0.999 * moment_two + 0.001 * rank_grad * rank_grad
    first_hat = new_one / (1.0 - 0.9**STEP)
    second_hat = new_two / (1.0 - 0.999**STEP)
    normalized = (first_hat / (jnp.sqrt(second_hat) + 1e-08)).astype(jnp.bfloat16)
    return (normalized, new_one, new_two)


def exchange(parts, axis):
    return lax.all_to_all(parts, axis, 0, 0)


def groups(axes, first, second):
    names = DP + TENSOR
    ids = np.arange(np.prod(SIZES)).reshape(SIZES)
    inside = [names.index(a) for a in axes]
    outside = [i for i in range(len(names)) if i not in inside]
    size = int(np.prod([SIZES[i] for i in inside]))
    lists = ids.transpose(outside + inside).reshape(-1, 2, size)
    return np.stack([lists[:, 0, first], lists[:, 1, second]], axis=1).reshape(-1, size).tolist()


def exchange_in(parts, axes, second, first=None):
    first = list(range(len(second))) if first is None else first
    return lax.all_to_all(
        parts, DP + TENSOR, 0, 0, axis_index_groups=groups(axes, first, second), tiled=True
    )


def turn(i):
    return i // SIZES[1] * SIZES[1] + (i + SIZES[1] // 2) % SIZES[1]


def ordered(out_grad, hidden, block):
    rows, width = out_grad.shape
    n = width // block
    n_zy, n_c = hidden.shape[:2]

    def kernel(out_grad_ref, hidden_ref, blocks_ref, tokens_ref, blocks, tokens, sems, out_sems):
        shift = lax.axis_index("c") * (SIZES[1] // 2)
        reads = []
        for i in range(n):
            at = i // SIZES[1] * SIZES[1] + lax.rem(i + shift, SIZES[1])
            columns = pl.ds(pl.multiple_of(at * block, block), block)
            reads.append((out_grad_ref.at[:, columns], blocks.at[i]))
        for i in range(n_zy):
            reads.append((hidden_ref.at[BY_YH[i], 0], tokens.at[0, i]))
        for i in range(n_zy):
            reads.append((hidden_ref.at[BY_YH[n_zy - 1 - i], 1], tokens.at[1, i]))
        reads = [pltpu.make_async_copy(*pair, sems.at[i]) for i, pair in enumerate(reads)]
        writes = [
            pltpu.make_async_copy(here, there, out_sems.at[i])
            for i, (here, there) in enumerate(
                ((blocks, blocks_ref), (tokens.at[0], tokens_ref.at[0]), (tokens.at[1], tokens_ref.at[1]))
            )
        ]
        for read in reads:
            read.start()
        for part, write in zip((reads[:n], reads[n : n + n_zy], reads[n + n_zy :]), writes):
            for read in part:
                read.wait()
            write.start()
        for write in writes:
            write.wait()

    whole = pl.BlockSpec(memory_space=pl.ANY)
    return pl.pallas_call(
        kernel,
        in_specs=[whole, whole],
        out_specs=[whole, whole],
        out_shape=[
            jax.ShapeDtypeStruct((n, rows, block), out_grad.dtype),
            jax.ShapeDtypeStruct((n_c, n_zy) + hidden.shape[2:], hidden.dtype),
        ],
        scratch_shapes=[
            pltpu.VMEM((n, rows, block), out_grad.dtype),
            pltpu.VMEM((n_c, n_zy) + hidden.shape[2:], hidden.dtype),
            pltpu.SemaphoreType.DMA((n + 2 * n_zy,)),
            pltpu.SemaphoreType.DMA((3,)),
        ],
        cost_estimate=pl.CostEstimate(
            flops=0, bytes_accessed=4 * (out_grad.size + hidden.size), transcendentals=0
        ),
    )(out_grad, hidden)


def summed(parts):
    return jnp.sum(parts.astype(jnp.float32), axis=0)


def shards(out_grad, hidden, projector, moment_one, moment_two):
    n_dp = lax.axis_size(DP)
    n_x, n_yl = lax.axis_size("x"), lax.axis_size("yl")
    n_zy = lax.axis_size(("z", "yh"))
    rows, width = out_grad.shape
    block, rank = projector.shape
    own_rows, columns = moment_one.shape
    quarter = rank // n_x

    core = lax.axis_index("c")
    pieces, tokens = ordered(out_grad, hidden.reshape(n_zy, 2, rows, columns), block)

    tokens = lax.all_gather(tokens.reshape(-1, columns), "x", axis=0, tiled=True)

    turned = [turn(i) for i in range(n_dp)]

    pieces = exchange_in(pieces, DP, turned)
    partial = jnp.dot(
        pieces.reshape(n_dp * rows, block), projector, preferred_element_type=jnp.float32
    ).astype(jnp.bfloat16)
    partial = partial.reshape(n_x, n_yl, rows, n_x, quarter).transpose(3, 1, 0, 2, 4)
    partial = partial.reshape(n_dp, n_x * rows, quarter)
    own = summed(exchange_in(partial, DP, turned)).astype(jnp.bfloat16)

    mine = jnp.broadcast_to(own, (n_zy, n_x * rows, quarter))
    mine = exchange_in(mine, ("z", "yh"), BY_YH[::-1], BY_YH)
    mine, tokens = lax.optimization_barrier((mine, tokens))
    other = lax.ppermute(mine, "c", [(0, 1), (1, 0)])
    tokens = tokens.reshape(n_x, 2, n_zy * rows, columns)
    group = jnp.zeros((quarter, columns), jnp.float32)
    for at, left in ((core, mine), (1 - core, other)):
        left = left.reshape(n_zy, n_x, rows, quarter).swapaxes(0, 1)
        group = group + lax.dot_general(
            left.reshape(n_x, n_zy * rows, quarter),
            lax.dynamic_index_in_dim(tokens, at, 1, keepdims=False),
            (((0, 1), (0, 1)), ((), ())),
            preferred_element_type=jnp.float32,
        )
    group = group.astype(jnp.bfloat16)

    blocks = group.reshape(n_yl, own_rows, columns)
    blocks = jnp.where(core == 0, blocks, jnp.roll(blocks, -2, axis=0))
    blocks = exchange_in(blocks, ("yl",), [2, 3, 0, 1])
    rank_grad = summed(blocks)

    normalized, new_one, new_two = adam_moments(rank_grad, moment_one, moment_two)

    part = lax.all_gather(normalized, "yl", axis=0, tiled=True)
    full = exchange(jnp.broadcast_to(part, (n_x,) + part.shape), "x").reshape(rank, columns)
    update = lax.dot_general(
        full, projector, (((0,), (1,)), ((), ())), preferred_element_type=jnp.float32
    )
    return (update.astype(jnp.bfloat16), new_one, new_two)


def solution(mesh):
    fine = Mesh(mesh.devices.reshape(SIZES), DP + TENSOR)
    in_specs = (
        P(DP + TENSOR, None),
        P(DP, TENSOR),
        P(DP, None),
        P(DP, TENSOR),
        P(DP, TENSOR),
    )
    out_specs = (P(TENSOR, DP), P(DP, TENSOR), P(DP, TENSOR))
    return jax.shard_map(shards, mesh=fine, in_specs=in_specs, out_specs=out_specs, check_vma=False)
```

```python
import jax
import jax.numpy as jnp
import numpy as np
from jax import lax
from jax.experimental import pallas as pl
from jax.experimental.pallas import tpu as pltpu
from jax.sharding import Mesh
from jax.sharding import PartitionSpec as P

STEP = 1000

DP = ("x", "yl")
TENSOR = ("z", "yh", "c")
SIZES = (4, 4, 8, 2, 2)
BY_YH = [z * SIZES[3] + yh for yh in range(SIZES[3]) for z in range(SIZES[2])]


def adam_moments(rank_grad, moment_one, moment_two):
    new_one = 0.9 * moment_one + 0.1 * rank_grad
    new_two = 0.999 * moment_two + 0.001 * rank_grad * rank_grad
    first_hat = new_one / (1.0 - 0.9**STEP)
    second_hat = new_two / (1.0 - 0.999**STEP)
    normalized = (first_hat / (jnp.sqrt(second_hat) + 1e-08)).astype(jnp.bfloat16)
    return (normalized, new_one, new_two)


def exchange(parts, axis):
    return lax.all_to_all(parts, axis, 0, 0)


def groups(axes, first, second):
    names = DP + TENSOR
    ids = np.arange(np.prod(SIZES)).reshape(SIZES)
    inside = [names.index(a) for a in axes]
    outside = [i for i in range(len(names)) if i not in inside]
    size = int(np.prod([SIZES[i] for i in inside]))
    lists = ids.transpose(outside + inside).reshape(-1, 2, size)
    return np.stack([lists[:, 0, first], lists[:, 1, second]], axis=1).reshape(-1, size).tolist()


def exchange_in(parts, axes, second, first=None):
    first = list(range(len(second))) if first is None else first
    return lax.all_to_all(
        parts, DP + TENSOR, 0, 0, axis_index_groups=groups(axes, first, second), tiled=True
    )


def turn(i):
    return i // SIZES[1] * SIZES[1] + (i + SIZES[1] // 2) % SIZES[1]


def ordered(out_grad, hidden, block):
    rows, width = out_grad.shape
    n = width // block
    n_zy, n_c = hidden.shape[:2]

    def kernel(out_grad_ref, hidden_ref, blocks_ref, tokens_ref, blocks, tokens, sems, out_sems):
        shift = lax.axis_index("c") * (SIZES[1] // 2)
        reads = []
        for i in range(n_zy):
            reads.append((hidden_ref.at[BY_YH[i], 0], tokens.at[0, i]))
        for i in range(n_zy):
            reads.append((hidden_ref.at[BY_YH[n_zy - 1 - i], 1], tokens.at[1, i]))
        for i in range(n):
            at = i // SIZES[1] * SIZES[1] + lax.rem(i + shift, SIZES[1])
            columns = pl.ds(pl.multiple_of(at * block, block), block)
            reads.append((out_grad_ref.at[:, columns], blocks.at[i]))
        reads = [pltpu.make_async_copy(*pair, sems.at[i]) for i, pair in enumerate(reads)]
        writes = [
            pltpu.make_async_copy(here, there, out_sems.at[i])
            for i, (here, there) in enumerate(
                ((tokens.at[0], tokens_ref.at[0]), (tokens.at[1], tokens_ref.at[1]), (blocks, blocks_ref))
            )
        ]
        for read in reads:
            read.start()
        for part, write in zip((reads[:n_zy], reads[n_zy : 2 * n_zy], reads[2 * n_zy :]), writes):
            for read in part:
                read.wait()
            write.start()
        for write in writes:
            write.wait()

    whole = pl.BlockSpec(memory_space=pl.ANY)
    return pl.pallas_call(
        kernel,
        in_specs=[whole, whole],
        out_specs=[whole, whole],
        out_shape=[
            jax.ShapeDtypeStruct((n, rows, block), out_grad.dtype),
            jax.ShapeDtypeStruct((n_c, n_zy) + hidden.shape[2:], hidden.dtype),
        ],
        scratch_shapes=[
            pltpu.VMEM((n, rows, block), out_grad.dtype),
            pltpu.VMEM((n_c, n_zy) + hidden.shape[2:], hidden.dtype),
            pltpu.SemaphoreType.DMA((n + 2 * n_zy,)),
            pltpu.SemaphoreType.DMA((3,)),
        ],
        cost_estimate=pl.CostEstimate(
            flops=0, bytes_accessed=4 * (out_grad.size + hidden.size), transcendentals=0
        ),
    )(out_grad, hidden)


def summed(parts):
    return jnp.sum(parts.astype(jnp.float32), axis=0)


def shards(out_grad, hidden, projector, moment_one, moment_two):
    n_dp = lax.axis_size(DP)
    n_x, n_yl = lax.axis_size("x"), lax.axis_size("yl")
    n_zy = lax.axis_size(("z", "yh"))
    rows, width = out_grad.shape
    block, rank = projector.shape
    own_rows, columns = moment_one.shape
    quarter = rank // n_x

    core = lax.axis_index("c")
    pieces, tokens = ordered(out_grad, hidden.reshape(n_zy, 2, rows, columns), block)

    tokens = lax.all_gather(tokens.reshape(-1, columns), "x", axis=0, tiled=True)

    turned = [turn(i) for i in range(n_dp)]

    pieces = exchange_in(pieces, DP, turned)
    pieces = pieces.reshape(n_dp * rows, block)
    partial = [
        jnp.dot(
            pieces, projector[:, i * quarter : (i + 1) * quarter], preferred_element_type=jnp.float32
        ).astype(jnp.bfloat16)
        for i in range(n_x)
    ]
    partial = jnp.stack(partial).reshape(n_x, n_x, n_yl, rows, quarter).swapaxes(1, 2)
    partial = partial.reshape(n_dp, n_x * rows, quarter)
    own = summed(exchange_in(partial, DP, turned)).astype(jnp.bfloat16)

    mine = jnp.broadcast_to(own, (n_zy, n_x * rows, quarter))
    mine = exchange_in(mine, ("z", "yh"), BY_YH[::-1], BY_YH)
    mine, tokens = lax.optimization_barrier((mine, tokens))
    other = lax.ppermute(mine, "c", [(0, 1), (1, 0)])
    tokens = tokens.reshape(n_x, 2, n_zy * rows, columns)
    group = jnp.zeros((quarter, columns), jnp.float32)
    for at, left in ((core, mine), (1 - core, other)):
        left = left.reshape(n_zy, n_x, rows, quarter).swapaxes(0, 1)
        group = group + lax.dot_general(
            left.reshape(n_x, n_zy * rows, quarter),
            lax.dynamic_index_in_dim(tokens, at, 1, keepdims=False),
            (((0, 1), (0, 1)), ((), ())),
            preferred_element_type=jnp.float32,
        )
    group = group.astype(jnp.bfloat16)

    blocks = group.reshape(n_yl, own_rows, columns)
    blocks = jnp.where(core == 0, blocks, jnp.roll(blocks, -2, axis=0))
    blocks = exchange_in(blocks, ("yl",), [2, 3, 0, 1])
    rank_grad = summed(blocks)

    normalized, new_one, new_two = adam_moments(rank_grad, moment_one, moment_two)

    part = lax.all_gather(normalized, "yl", axis=0, tiled=True)
    full = exchange(jnp.broadcast_to(part, (n_x,) + part.shape), "x").reshape(rank, columns)
    update = lax.dot_general(
        full, projector, (((0,), (1,)), ((), ())), preferred_element_type=jnp.float32
    )
    return (update.astype(jnp.bfloat16), new_one, new_two)


def solution(mesh):
    fine = Mesh(mesh.devices.reshape(SIZES), DP + TENSOR)
    in_specs = (
        P(DP + TENSOR, None),
        P(DP, TENSOR),
        P(DP, None),
        P(DP, TENSOR),
        P(DP, TENSOR),
    )
    out_specs = (P(TENSOR, DP), P(DP, TENSOR), P(DP, TENSOR))
    return jax.shard_map(shards, mesh=fine, in_specs=in_specs, out_specs=out_specs, check_vma=False)
```
